256 devices in a mesh: pair: 16 (over y_hi, z), row: 4 (over x), col: 4 (over y_lo, core).
Axes of the slice: x: 4, y: 4 (y_hi: 2, y_lo: 2; y = y_hi * 2 + y_lo), z: 8, core: 2. Of those that a mesh axis runs over, the one named last changes fastest.
Arguments:
- psi_val: bfloat16 [32, 786432], P(None, ('row', 'col')), may hold values from -6 to 6
- psi_con: bfloat16 [64, 786432], P(None, ('row', 'col')), may hold values from -6 to 6
- e_val: float32 [32], replicated, may hold values from -12 to -2
- e_con: float32 [64], replicated, may hold values from 1 to 10
- val_idx: int32 [512], P('pair'), may hold values from 0 to 31
- con_idx: int32 [512], P('pair'), may hold values from 0 to 63
- gmap: int32 [4096], replicated, may hold values from 0 to 786431, as said below
Outputs:
- chi: float32 [4096, 4096], P(('pair', 'row'), 'col')
The draws below stay inside these ranges and needn't reach their ends.
Inputs may be any that keep to these rules, and one draw needn't show every extreme that they name: `gmap`: distinct grid indices; both 0 and 786431 occur.
All inputs are finite; a program needn't handle non-finite values.
Results may differ from the reference program's by a relative error of at most 0.0059.
Values may be sent and summed in bfloat16 or wider, within the bound.
No kernel may reach another device: no remote copies, remote signals or barrier semaphores. Data moves between devices by JAX's collectives and lax.ppermute only.
A program may use at most 192 MiB of HBM per device.

```python
import math
import jax
import jax.numpy as jnp
from jax import lax

NV = 32
NC = 64
NG = 4096
GX = 64
GY = 64
GZ = 192
PAIRS = 512
RGRID = 786432


def draw_gmap(key, part):
    key = jax.random.fold_in(key, 7)
    first, second = jax.random.split(key)
    total = GX * GY * GZ
    inner = 1 + jax.random.permutation(first, total - 2)[:NG - 2]
    chosen = jnp.concatenate([jnp.zeros((1,), jnp.int32), inner.astype(jnp.int32), jnp.full((1,), total - 1, jnp.int32)])
    order = jax.random.permutation(second, NG)
    return chosen[order].astype(jnp.int32)


def place_ends(entries, rng, least, high):
    dims = entries.shape
    index_at = [jax.random.randint(jax.random.fold_in(rng, axis), (), 0, dims[axis]) for axis in range(len(dims))]
    entries = entries.at[tuple(index_at)].set(least)
    longest = dims.index(max(dims))
    index_at[longest] = (index_at[longest] + 1) % dims[longest]
    return entries.at[tuple(index_at)].set(high)


def levels(own_key, shape, pieces, low, top_value):
    gain = 1.0
    for dim, parts in pieces:
        draws = jax.random.uniform(jax.random.fold_in(jax.random.fold_in(own_key, 6), dim), (parts,), jnp.float32, low / len(pieces), top_value / len(pieces))
        gain = gain * jnp.repeat(jnp.exp(draws), shape[dim] // parts).reshape((-1,) + (1,) * (len(shape) - 1 - dim))
    return gain


def normal_values(stream_key, extent, spread, limit, cuts=(), kind=jnp.bfloat16):
    values = spread * jax.random.normal(stream_key, extent, jnp.float32)
    if cuts:
        values = values * levels(stream_key, extent, cuts, -0.22, 0.18)
    return jnp.clip(values, -limit, limit).astype(kind)


def setup_inputs(seed: int = 0) -> dict:
    keys = jax.random.split(jax.random.key(seed), 8)
    return {
        "psi_val": normal_values(keys[0], (NV, RGRID), 1.0, 6.0, ((1, 16),)),
        "psi_con": normal_values(keys[1], (NC, RGRID), 1.0, 6.0, ((1, 16),)),
        "e_val": jnp.clip(jax.random.uniform(keys[2], (NV,), jnp.float32, -12.0, -2.0), -12.0, -2.0),
        "e_con": jnp.clip(jax.random.uniform(keys[3], (NC,), jnp.float32, 1.0, 10.0), 1.0, 10.0),
        "val_idx": place_ends(jax.random.randint(keys[4], (PAIRS,), 0, NV), jax.random.fold_in(keys[4], 1), 0, NV - 1).astype(jnp.int32),
        "con_idx": place_ends(jax.random.randint(keys[5], (PAIRS,), 0, NC), jax.random.fold_in(keys[5], 1), 0, NC - 1).astype(jnp.int32),
        "gmap": draw_gmap(jax.random.fold_in(keys[7], 71), 0),
    }


def reference(psi_val, psi_con, e_val, e_con, val_idx, con_idx, gmap):
    rho = (psi_val[val_idx].astype(jnp.float32) * psi_con[con_idx].astype(jnp.float32)).astype(jnp.bfloat16)
    weights = -2.0 / (math.sqrt(PAIRS) * (e_con[con_idx] - e_val[val_idx]))
    factor = 1.0 / math.sqrt(GX * GY * GZ)
    blocks = rho.reshape(PAIRS // 16, 16, GX, GY, GZ)

    def transform_block(block):
        spectrum = jnp.fft.fftn(block.astype(jnp.float32), axes=(1, 2, 3)).reshape(16, GX * GY * GZ)
        picked = jnp.take(spectrum, gmap, axis=1)
        stacked = jnp.stack((jnp.real(picked), jnp.imag(picked)), axis=2)
        return stacked.reshape(16, 2 * NG) * factor
    coeffs = lax.map(transform_block, blocks).reshape(PAIRS, 2 * NG)
    trans = coeffs.T.astype(jnp.bfloat16)
    weighted = (trans.astype(jnp.float32).reshape(NG, 2, PAIRS) * weights[None, None, :]).astype(jnp.bfloat16)
    weighted = weighted.reshape(NG, 2 * PAIRS)
    plain = trans.reshape(NG, 2 * PAIRS)
    return lax.dot_general(weighted, plain, (((1,), (1,)), ((), ())), preferred_element_type=jnp.float32)
```

```python
import math
import numpy as np
import jax, jax.numpy as jnp
from jax import lax
from jax.experimental import pallas as pl
from jax.experimental.pallas import tpu as pltpu
from jax.sharding import PartitionSpec as P
import ml_dtypes
BF=ml_dtypes.bfloat16
GX=64;GY=64;GZ=192;NG=4096
KZ=104

def split_hi_lo(t):
    hi=t.astype(np.float32).astype(BF); lo=(t-hi.astype(np.float64)).astype(np.float32).astype(BF)
    return hi,lo

def z_tables():
    z=np.arange(GZ); k=np.arange(97)
    ang=2*np.pi/GZ*((k[:,None]*z[None,:])%GZ)
    t=np.zeros((2,KZ,GZ)); t[0,:97]=np.cos(ang); t[1,:97]=-np.sin(ang)
    t=t.reshape(2*KZ,GZ)
    out=np.zeros((2,2*KZ,512),BF)
    hi,lo=split_hi_lo(t)
    for par,off in ((0,0),(1,64)):
        out[par,:,off:off+GZ]=hi; out[par,:,256+off:256+off+GZ]=lo
    return out

def x_tables():
    factor=1.0/math.sqrt(GX*GY*GZ)
    out=np.zeros((16,256,512),BF)
    fx=np.arange(64)
    for d in range(16):
        xs=4*d+np.arange(4)
        ang=2*np.pi/GX*((fx[:,None]*xs[None,:])%GX)
        c=np.repeat(np.cos(ang),32,axis=1)*factor; s=np.repeat(np.sin(ang),32,axis=1)*factor
        for f,sig in ((0,1.0),(1,-1.0)):
            t=np.concatenate([c,sig*s,sig*c,-s],axis=1)
            hi,lo=split_hi_lo(t)
            out[d,f*64:(f+1)*64]=hi; out[d,128+f*64:128+(f+1)*64]=lo
    return out

def fft8(v):
    def add(a,b): return (a[0]+b[0],a[1]+b[1])
    def sub(a,b): return (a[0]-b[0],a[1]-b[1])
    def mi(a): return (a[1],-a[0])
    r=np.float32(math.sqrt(0.5))
    def fft4(x0,x1,x2,x3):
        a=add(x0,x2); b=sub(x0,x2); c=add(x1,x3); d=mi(sub(x1,x3))
        return add(a,c),add(b,d),sub(a,c),sub(b,d)
    e=fft4(v[0],v[2],v[4],v[6]); o=fft4(v[1],v[3],v[5],v[7])
    o1=((o[1][0]+o[1][1])*r,(o[1][1]-o[1][0])*r)
    o2=mi(o[2])
    o3=((o[3][1]-o[3][0])*r,-(o[3][0]+o[3][1])*r)
    os=(o[0],o1,o2,o3)
    return [add(e[k],os[k]) for k in range(4)]+[sub(e[k],os[k]) for k in range(4)]

def transform_kernel(val_s, con_s, row_s, dev_s, pv, pc, kcode, ztab, xtab, out, rho, Z, Z2, GA, GB):
    step=pl.program_id(0)
    sub=lax.broadcasted_iota(jnp.int32,(64,96),0); lane=lax.broadcasted_iota(jnp.int32,(64,96),1)
    want=jnp.zeros((64,96),jnp.int32)
    for p in range(32):
        want=jnp.where(sub==p, val_s[p], want)
        want=jnp.where(sub==32+p, con_s[p]+32, want)
    sel=(want==lane).astype(jnp.bfloat16)
    CH=512; NU=24
    def rho_body(i,_):
        for u in range(NU):
            o=pl.multiple_of(i*(CH*NU)+u*CH,CH)
            src=jnp.concatenate([pv[:,pl.ds(o,CH)],pc[:,pl.ds(o,CH)]],axis=0)
            res=jnp.dot(sel,src,preferred_element_type=jnp.float32)
            rho[step,:,pl.ds(o,CH)]=(res[:32]*res[32:]).astype(jnp.bfloat16)
        return 0
    lax.fori_loop(0,12288//(CH*NU),rho_body,0)

    @pl.when(step==3)
    def _():
        for b in range(8):
            wt=ztab[b%2]
            for ah in range(4):
                parts=[]
                for a in (2*ah,2*ah+1):
                    yp=4*a+b//2; o=384*yp+128*(b%2)
                    for x in range(4):
                        parts.append(rho[x,:,o:o+256])
                B=jnp.concatenate(parts,axis=0)
                B=jnp.concatenate([B,B],axis=1)
                res=lax.dot_general(wt,B,(((1,),(1,)),((),())),preferred_element_type=jnp.float32)
                Z[pl.ds((8*(2*ah)+b)*2*KZ,2*KZ),:]=res[:,:128]
                Z[pl.ds((8*(2*ah+1)+b)*2*KZ,2*KZ),:]=res[:,128:]
        tw=[[np.exp(-2j*np.pi*b*k/64) for k in range(8)] for b in range(8)]
        def pass1(j,_):
            r0=pl.multiple_of(j*8,8)
            for b in range(8):
                v=[(Z[pl.ds((8*a+b)*2*KZ+r0,8),:],Z[pl.ds((8*a+b)*2*KZ+KZ+r0,8),:]) for a in range(8)]
                w=fft8(v)
                for k in range(8):
                    re,im=w[k]
                    if b and k:
                        c=np.float32(tw[b][k].real); s=np.float32(tw[b][k].imag)
                        re,im=re*c-im*s, re*s+im*c
                    Z[pl.ds((8*k+b)*2*KZ+r0,8),:]=re; Z[pl.ds((8*k+b)*2*KZ+KZ+r0,8),:]=im
            return 0
        lax.fori_loop(0,KZ//8,pass1,0)
        def pass2(j,_):
            r0=pl.multiple_of(j*8,8)
            for k1 in range(8):
                v=[(Z[pl.ds((8*k1+b)*2*KZ+r0,8),:],Z[pl.ds((8*k1+b)*2*KZ+KZ+r0,8),:]) for b in range(8)]
                w=fft8(v)
                for k in range(8):
                    re,im=w[k]
                    base=(8*k1+k)*2*KZ+2*r0
                    Z2[pl.ds(base,8,stride=2),:]=re; Z2[pl.ds(base+1,8,stride=2),:]=im
            return 0
        lax.fori_loop(0,KZ//8,pass2,0)
        ksub=lax.broadcasted_iota(jnp.int32,(128,256),0)
        ln=lax.broadcasted_iota(jnp.int32,(128,128),1)
        lnb=lax.broadcasted_iota(jnp.int32,(256,128),1)
        def gather(t,G):
            base=t*256
            for j in range(256):
                rr=pl.multiple_of(row_s[base+j],2)
                G[pl.ds(2*j,2),:]=Z2[pl.ds(rr,2),:]
        def phase(t,G):
            base=t*256
            code=kcode[:,pl.ds(pl.multiple_of(base,256),256)]
            oh=(ksub==code).astype(jnp.bfloat16)
            oh=jnp.concatenate([oh,oh],axis=0)
            co=lax.dot_general(oh,xtab[0],(((0,),(0,)),((),())),preferred_element_type=jnp.float32)
            R=G[pl.ds(0,256,stride=2),:]; I=G[pl.ds(1,256,stride=2),:]
            re=co[:,:128]*R+co[:,128:256]*I
            im=co[:,256:384]*I+co[:,384:]*R
            t1=re+pltpu.roll(re,64,1); u1=im+pltpu.roll(im,64,1)
            w=jnp.where(lnb<64,t1,u1)
            w0=w[:128]; w1=w[128:]
            v0=w0+pltpu.roll(w0,96,1)
            v1=w1+pltpu.roll(w1,32,1)
            out[(t%4)*4+t//4]=jnp.where((ln%64)<32,v0,v1).astype(jnp.bfloat16)
        gather(0,GA)
        def pairs(u,_):
            t=2*u
            gather(t+1,GB); phase(t,GA)
            gather(jnp.minimum(t+2,15),GA); phase(t+1,GB)
            return 0
        lax.fori_loop(0,8,pairs,0)

def prep(gmap):
    fz=gmap%GZ; q=gmap//GZ; fy=q%GY; fx=q//GY
    flag=(fz>96).astype(jnp.int32)
    fz2=jnp.where(fz>96,GZ-fz,fz); fy2=jnp.where(fz>96,(GY-fy)%GY,fy)
    loc=8*(fy2%8)+fy2//8
    rows=loc*(2*KZ)+2*fz2
    return rows, (flag*64+fx)

def kernel1(val_idx,con_idx,rows,code,dev,pv,pc):
    return pl.pallas_call(
        transform_kernel,
        grid_spec=pltpu.PrefetchScalarGridSpec(
            num_scalar_prefetch=4, grid=(4,),
            in_specs=[pl.BlockSpec((32,12288),lambda i,*_:(0,i)),
                      pl.BlockSpec((64,12288),lambda i,*_:(0,i)),
                      pl.BlockSpec((1,NG),lambda i,*_:(0,0)),
                      pl.BlockSpec((2,2*KZ,512),lambda i,*_:(0,0,0)),
                      pl.BlockSpec((1,256,512),lambda i,a,b,c,d:(d[0],0,0))],
            out_specs=pl.BlockSpec((16,128,128),lambda i,*_:(0,0,0)),
            scratch_shapes=[pltpu.VMEM((4,32,12288),jnp.bfloat16),
                            pltpu.VMEM((64*2*KZ,128),jnp.float32),
                            pltpu.VMEM((64*2*KZ,128),jnp.float32),pltpu.VMEM((512,128),jnp.float32),pltpu.VMEM((512,128),jnp.float32)]),
        out_shape=jax.ShapeDtypeStruct((16,128,128),jnp.bfloat16),
        compiler_params=pltpu.CompilerParams(vmem_limit_bytes=48*2**20, dimension_semantics=("arbitrary",)),
        name="partial_transform",
    )(val_idx,con_idx,rows,dev,pv,pc,code.reshape(1,NG),jnp.asarray(z_tables()),jnp.asarray(x_tables()))


def sum_kernel(val_s,con_s,ev_s,ec_s,recv,out):
    acc=recv[0].astype(jnp.float32)
    for i in range(1,16):
        acc=acc+recv[i].astype(jnp.float32)
    pid=lax.broadcasted_iota(jnp.int32,(16,128),1)%32
    ev=jnp.zeros((16,128),jnp.float32); ec=jnp.ones((16,128),jnp.float32)
    for p in range(32):
        ev=jnp.where(pid==p,ev_s[val_s[p]],ev)
        ec=jnp.where(pid==p,ec_s[con_s[p]],ec)
    w=-2.0/(math.sqrt(512)*(ec-ev))
    hi=w.astype(jnp.bfloat16).astype(jnp.float32)
    mid=(w-hi).astype(jnp.bfloat16).astype(jnp.float32)
    lo=w-hi-mid
    row=lax.broadcasted_iota(jnp.int32,(16,128),0)
    wr=jnp.where(row==0,hi,jnp.where(row==1,mid,lo)).astype(jnp.bfloat16)
    full=jnp.concatenate([acc.astype(jnp.bfloat16),wr],axis=0)
    for i in range(16):
        out[i]=full

def tile_kernel(t,rw,out,lhs):
    half=lax.axis_index("row")//2
    ln=lax.broadcasted_iota(jnp.int32,(64,128),1)
    first=(ln%64)<32
    for g in range(16):
        w=t[0,g,128:144,:].astype(jnp.float32)
        w=w[0:1]+w[1:2]+w[2:3]
        d=rw[g].astype(jnp.float32)
        d=jnp.where(half==1,pltpu.roll(d,96,1),d)
        d=jnp.where(first,d*w,0.0)
        lhs[g,0:64,:]=d.astype(jnp.bfloat16)
        lhs[g,64:128,:]=pltpu.roll(d,32,1).astype(jnp.bfloat16)
    for r in range(4):
        acc=jnp.zeros((128,128),jnp.float32)
        for g in range(16):
            acc=acc+lax.dot_general(lhs[g],t[r,g,0:128,:],(((1,),(1,)),((),())),preferred_element_type=jnp.float32)
        out[:,256*r:256*r+128]=acc[:64]
        out[:,256*r+128:256*r+256]=acc[64:]

SMEM=pl.BlockSpec(memory_space=pltpu.SMEM)
VM=pl.BlockSpec(memory_space=pltpu.VMEM)

def body(psi_val, psi_con, e_val, e_con, val_idx, con_idx, gmap):
    pair=lax.axis_index("pair"); row=lax.axis_index("row"); col=lax.axis_index("col")
    rows,code=prep(gmap)
    part=kernel1(val_idx,con_idx,rows,code,(row*4+col).reshape(1),psi_val,psi_con)
    recv=lax.all_to_all(part,("row","col"),split_axis=0,concat_axis=0,tiled=True)
    payload=pl.pallas_call(sum_kernel,in_specs=[SMEM]*4+[VM],out_specs=VM,
        out_shape=jax.ShapeDtypeStruct((16,144,128),jnp.bfloat16),name="sum_parts")(val_idx,con_idx,e_val,e_con,recv)
    groups=lax.all_to_all(payload,"pair",split_axis=0,concat_axis=0,tiled=True)
    perm=[]
    for p in range(16):
        for r in range(4):
            for c in range(4):
                perm.append(((r*4+c)*16+(p%4)*4+p//4, p*16+r*4+c))
    piece=lax.dynamic_slice_in_dim(groups,((pair//4)%2)*64,64,1)
    rowpart=lax.ppermute(piece,("pair","row","col"),perm)
    full=lax.all_gather(groups,"row",axis=0)
    return pl.pallas_call(tile_kernel,in_specs=[VM,VM],out_specs=VM,
        out_shape=jax.ShapeDtypeStruct((64,1024),jnp.float32),
        scratch_shapes=[pltpu.VMEM((16,128,128),jnp.bfloat16)],
        compiler_params=pltpu.CompilerParams(vmem_limit_bytes=16*2**20),
        name="tile")(full,rowpart)

def solution(mesh):
    return jax.shard_map(
        body,
        mesh=mesh,
        in_specs=(
            P(None, ("row", "col")),
            P(None, ("row", "col")),
            P(),
            P(),
            P("pair"),
            P("pair"),
            P(),
        ),
        out_specs=P(("pair", "row"), "col"),
        check_vma=False,
    )
```

```python
import math
import numpy as np
import jax, jax.numpy as jnp
from jax import lax
from jax.experimental import pallas as pl
from jax.experimental.pallas import tpu as pltpu
from jax.sharding import PartitionSpec as P
import ml_dtypes
BF=ml_dtypes.bfloat16
GX=64;GY=64;GZ=192;NG=4096
KZ=104

def split_hi_lo(t):
    hi=t.astype(np.float32).astype(BF); lo=(t-hi.astype(np.float64)).astype(np.float32).astype(BF)
    return hi,lo

def z_tables():
    z=np.arange(GZ); k=np.arange(97)
    ang=2*np.pi/GZ*((k[:,None]*z[None,:])%GZ)
    t=np.zeros((2,KZ,GZ)); t[0,:97]=np.cos(ang); t[1,:97]=-np.sin(ang)
    t=t.reshape(2*KZ,GZ)
    out=np.zeros((2,2*KZ,512),BF)
    hi,lo=split_hi_lo(t)
    for par,off in ((0,0),(1,64)):
        out[par,:,off:off+GZ]=hi; out[par,:,256+off:256+off+GZ]=lo
    return out

def x_tables():
    factor=1.0/math.sqrt(GX*GY*GZ)
    out=np.zeros((16,256,512),BF)
    fx=np.arange(64)
    for d in range(16):
        xs=4*d+np.arange(4)
        ang=2*np.pi/GX*((fx[:,None]*xs[None,:])%GX)
        c=np.repeat(np.cos(ang),32,axis=1)*factor; s=np.repeat(np.sin(ang),32,axis=1)*factor
        for f,sig in ((0,1.0),(1,-1.0)):
            t=np.concatenate([c,sig*s,sig*c,-s],axis=1)
            hi,lo=split_hi_lo(t)
            out[d,f*64:(f+1)*64]=hi; out[d,128+f*64:128+(f+1)*64]=lo
    return out

def fft8(v):
    def add(a,b): return (a[0]+b[0],a[1]+b[1])
    def sub(a,b): return (a[0]-b[0],a[1]-b[1])
    def mi(a): return (a[1],-a[0])
    r=np.float32(math.sqrt(0.5))
    def fft4(x0,x1,x2,x3):
        a=add(x0,x2); b=sub(x0,x2); c=add(x1,x3); d=mi(sub(x1,x3))
        return add(a,c),add(b,d),sub(a,c),sub(b,d)
    e=fft4(v[0],v[2],v[4],v[6]); o=fft4(v[1],v[3],v[5],v[7])
    o1=((o[1][0]+o[1][1])*r,(o[1][1]-o[1][0])*r)
    o2=mi(o[2])
    o3=((o[3][1]-o[3][0])*r,-(o[3][0]+o[3][1])*r)
    os=(o[0],o1,o2,o3)
    return [add(e[k],os[k]) for k in range(4)]+[sub(e[k],os[k]) for k in range(4)]

def transform_kernel(val_s, con_s, row_s, pv, pc, kcode, ztab, xtabs, out, rho, Z, Z2, GA, GB, xtab, xsem):
    step=pl.program_id(0)
    place=lax.axis_index("row")*4+lax.axis_index("col")
    fetch=pltpu.make_async_copy(xtabs.at[place],xtab,xsem)
    @pl.when(step==0)
    def _():
        fetch.start()
    sub=lax.broadcasted_iota(jnp.int32,(64,96),0); lane=lax.broadcasted_iota(jnp.int32,(64,96),1)
    want=jnp.zeros((64,96),jnp.int32)
    for p in range(32):
        want=jnp.where(sub==p, val_s[p], want)
        want=jnp.where(sub==32+p, con_s[p]+32, want)
    sel=(want==lane).astype(jnp.bfloat16)
    CH=512; NU=24
    def rho_body(i,_):
        for u in range(NU):
            o=pl.multiple_of(i*(CH*NU)+u*CH,CH)
            src=jnp.concatenate([pv[:,pl.ds(o,CH)],pc[:,pl.ds(o,CH)]],axis=0)
            res=jnp.dot(sel,src,preferred_element_type=jnp.float32)
            rho[step,:,pl.ds(o,CH)]=(res[:32]*res[32:]).astype(jnp.bfloat16)
        return 0
    lax.fori_loop(0,12288//(CH*NU),rho_body,0)

    @pl.when(step==3)
    def _():
        fetch.wait()
        for b in range(8):
            wt=ztab[b%2]
            for ah in range(4):
                parts=[]
                for a in (2*ah,2*ah+1):
                    yp=4*a+b//2; o=384*yp+128*(b%2)
                    for x in range(4):
                        parts.append(rho[x,:,o:o+256])
                B=jnp.concatenate(parts,axis=0)
                B=jnp.concatenate([B,B],axis=1)
                res=lax.dot_general(wt,B,(((1,),(1,)),((),())),preferred_element_type=jnp.float32)
                Z[pl.ds((8*(2*ah)+b)*2*KZ,2*KZ),:]=res[:,:128]
                Z[pl.ds((8*(2*ah+1)+b)*2*KZ,2*KZ),:]=res[:,128:]
        tw=[[np.exp(-2j*np.pi*b*k/64) for k in range(8)] for b in range(8)]
        def pass1(j,_):
            r0=pl.multiple_of(j*8,8)
            for b in range(8):
                v=[(Z[pl.ds((8*a+b)*2*KZ+r0,8),:],Z[pl.ds((8*a+b)*2*KZ+KZ+r0,8),:]) for a in range(8)]
                w=fft8(v)
                for k in range(8):
                    re,im=w[k]
                    if b and k:
                        c=np.float32(tw[b][k].real); s=np.float32(tw[b][k].imag)
                        re,im=re*c-im*s, re*s+im*c
                    Z[pl.ds((8*k+b)*2*KZ+r0,8),:]=re; Z[pl.ds((8*k+b)*2*KZ+KZ+r0,8),:]=im
            return 0
        lax.fori_loop(0,KZ//8,pass1,0)
        def pass2(j,_):
            r0=pl.multiple_of(j*8,8)
            for k1 in range(8):
                v=[(Z[pl.ds((8*k1+b)*2*KZ+r0,8),:],Z[pl.ds((8*k1+b)*2*KZ+KZ+r0,8),:]) for b in range(8)]
                w=fft8(v)
                for k in range(8):
                    re,im=w[k]
                    base=(8*k1+k)*2*KZ+2*r0
                    Z2[pl.ds(base,8,stride=2),:]=re; Z2[pl.ds(base+1,8,stride=2),:]=im
            return 0
        lax.fori_loop(0,KZ//8,pass2,0)
        ksub=lax.broadcasted_iota(jnp.int32,(128,256),0)
        ln=lax.broadcasted_iota(jnp.int32,(128,128),1)
        lnb=lax.broadcasted_iota(jnp.int32,(256,128),1)
        def gather(t,G):
            base=t*256
            for j in range(256):
                rr=pl.multiple_of(row_s[base+j],2)
                G[pl.ds(2*j,2),:]=Z2[pl.ds(rr,2),:]
        def phase(t,G):
            base=t*256
            code=kcode[:,pl.ds(pl.multiple_of(base,256),256)]
            oh=(ksub==code).astype(jnp.bfloat16)
            oh=jnp.concatenate([oh,oh],axis=0)
            co=lax.dot_general(oh,xtab[...],(((0,),(0,)),((),())),preferred_element_type=jnp.float32)
            R=G[pl.ds(0,256,stride=2),:]; I=G[pl.ds(1,256,stride=2),:]
            re=co[:,:128]*R+co[:,128:256]*I
            im=co[:,256:384]*I+co[:,384:]*R
            t1=re+pltpu.roll(re,64,1); u1=im+pltpu.roll(im,64,1)
            w=jnp.where(lnb<64,t1,u1)
            w0=w[:128]; w1=w[128:]
            v0=w0+pltpu.roll(w0,96,1)
            v1=w1+pltpu.roll(w1,32,1)
            o=jnp.where((ln%64)<32,v0,v1).T
            c=t//4
            for h in range(2):
                at=pl.multiple_of((t%4)*256+h*128,128)
                for r in range(4):
                    lo=h*32+r*8
                    both=jnp.concatenate([o[lo:lo+8],o[64+lo:64+lo+8]],axis=0)
                    out[r*4+c,:,pl.ds(at,128)]=both.astype(jnp.bfloat16)
        gather(0,GA)
        def pairs(u,_):
            t=2*u
            gather(t+1,GB); phase(t,GA)
            gather(jnp.minimum(t+2,15),GA); phase(t+1,GB)
            return 0
        lax.fori_loop(0,8,pairs,0)

def prep(gmap):
    fz=gmap%GZ; q=gmap//GZ; fy=q%GY; fx=q//GY
    flag=(fz>96).astype(jnp.int32)
    fz2=jnp.where(fz>96,GZ-fz,fz); fy2=jnp.where(fz>96,(GY-fy)%GY,fy)
    loc=8*(fy2%8)+fy2//8
    rows=loc*(2*KZ)+2*fz2
    return rows, (flag*64+fx)

def kernel1(val_idx,con_idx,rows,code,pv,pc):
    smem=pl.BlockSpec(memory_space=pltpu.SMEM)
    return pl.pallas_call(
        transform_kernel,
        grid=(4,),
        in_specs=[smem,smem,smem,
                  pl.BlockSpec((32,12288),lambda i:(0,i)),
                  pl.BlockSpec((64,12288),lambda i:(0,i)),
                  pl.BlockSpec((1,NG),lambda i:(0,0)),
                  pl.BlockSpec((2,2*KZ,512),lambda i:(0,0,0)),
                  pl.BlockSpec(memory_space=pl.ANY)],
        out_specs=pl.BlockSpec((16,16,1024),lambda i:(0,0,0)),
        scratch_shapes=[pltpu.VMEM((4,32,12288),jnp.bfloat16),
                        pltpu.VMEM((64*2*KZ,128),jnp.float32),
                        pltpu.VMEM((64*2*KZ,128),jnp.float32),
                        pltpu.VMEM((512,128),jnp.float32),
                        pltpu.VMEM((512,128),jnp.float32),
                        pltpu.VMEM((256,512),jnp.bfloat16),
                        pltpu.SemaphoreType.DMA],
        out_shape=jax.ShapeDtypeStruct((16,16,1024),jnp.bfloat16),
        compiler_params=pltpu.CompilerParams(vmem_limit_bytes=60*2**20, dimension_semantics=("arbitrary",)),
        name="partial_transform",
    )(val_idx,con_idx,rows,pv,pc,code.reshape(1,NG),jnp.asarray(z_tables()),jnp.asarray(x_tables()))

def sum_kernel(parts,out):
    acc=parts[0].astype(jnp.float32)
    for i in range(1,16):
        acc=acc+parts[i].astype(jnp.float32)
    out[...]=acc.astype(jnp.bfloat16)

def payload_kernel(val_s,con_s,ev_s,ec_s,own,every,out):
    first=lax.axis_index("row")*8
    pid=lax.broadcasted_iota(jnp.int32,(16,256),0)%8
    ev=jnp.zeros((16,256),jnp.float32); ec=jnp.ones((16,256),jnp.float32)
    for p in range(8):
        ev=jnp.where(pid==p,ev_s[val_s[first+p]],ev)
        ec=jnp.where(pid==p,ec_s[con_s[first+p]],ec)
    w=-2.0/(math.sqrt(512)*(ec-ev))
    mine=own[...]
    for p in range(16):
        out[p,:,0:1024]=mine
        rows=every[p//4,:,256*(p%4):256*(p%4)+256].astype(jnp.float32)
        out[p,:,1024:1280]=(rows*w).astype(jnp.bfloat16)

def tile_kernel(t,out):
    left=t[:,1024:1280].astype(jnp.float32).T.astype(jnp.bfloat16)
    for n in range(4):
        part=jnp.dot(left,t[:,256*n:256*n+256],preferred_element_type=jnp.float32)
        for r in range(4):
            out[r,:,256*n:256*n+256]=part[64*r:64*r+64].astype(out.dtype)

def final_kernel(parts,out):
    acc=parts[0].astype(jnp.float32)
    for i in range(1,4):
        acc=acc+parts[i].astype(jnp.float32)
    out[...]=acc

SMEM=pl.BlockSpec(memory_space=pltpu.SMEM)
VM=pl.BlockSpec(memory_space=pltpu.VMEM)
SEND=jnp.bfloat16

def body(psi_val, psi_con, e_val, e_con, val_idx, con_idx, gmap):
    rows,code=prep(gmap)
    part=kernel1(val_idx,con_idx,rows,code,psi_val,psi_con)
    recv=lax.all_to_all(part,("row","col"),split_axis=0,concat_axis=0,tiled=True)
    own=pl.pallas_call(sum_kernel,in_specs=[VM],out_specs=VM,
        out_shape=jax.ShapeDtypeStruct((16,1024),jnp.bfloat16),name="sum_parts")(recv)
    every=lax.all_gather(own,"col",axis=0)
    payload=pl.pallas_call(payload_kernel,in_specs=[SMEM]*4+[VM]*2,out_specs=VM,
        out_shape=jax.ShapeDtypeStruct((16,16,1280),jnp.bfloat16),name="payload")(val_idx,con_idx,e_val,e_con,own,every)
    groups=lax.all_to_all(payload,"pair",split_axis=0,concat_axis=0,tiled=True)
    tiles=pl.pallas_call(tile_kernel,in_specs=[VM],out_specs=VM,
        out_shape=jax.ShapeDtypeStruct((4,64,1024),SEND),name="tile")(groups.reshape(256,1280))
    tiles=lax.all_to_all(tiles,"row",split_axis=0,concat_axis=0,tiled=True)
    return pl.pallas_call(final_kernel,in_specs=[VM],out_specs=VM,
        out_shape=jax.ShapeDtypeStruct((64,1024),jnp.float32),name="total")(tiles)

def solution(mesh):
    return jax.shard_map(
        body,
        mesh=mesh,
        in_specs=(
            P(None, ("row", "col")),
            P(None, ("row", "col")),
            P(),
            P(),
            P("pair"),
            P("pair"),
            P(),
        ),
        out_specs=P(("pair", "row"), "col"),
        check_vma=False,
    )
```

```python
import math
import numpy as np
import jax, jax.numpy as jnp
from jax import lax
from jax.experimental import pallas as pl
from jax.experimental.pallas import tpu as pltpu
from jax.sharding import Mesh, PartitionSpec as P
import ml_dtypes
BF=ml_dtypes.bfloat16
GX=64;GY=64;GZ=192;NG=4096
KZ=104

def split_hi_lo(t):
    hi=t.astype(np.float32).astype(BF); lo=(t-hi.astype(np.float64)).astype(np.float32).astype(BF)
    return hi,lo

def z_tables():
    z=np.arange(GZ); k=np.arange(97)
    ang=2*np.pi/GZ*((k[:,None]*z[None,:])%GZ)
    t=np.zeros((2,KZ,GZ)); t[0,:97]=np.cos(ang); t[1,:97]=-np.sin(ang)
    t=t.reshape(2*KZ,GZ)
    out=np.zeros((2,2*KZ,512),BF)
    hi,lo=split_hi_lo(t)
    for par,off in ((0,0),(1,64)):
        out[par,:,off:off+GZ]=hi; out[par,:,256+off:256+off+GZ]=lo
    return out

def x_tables():
    factor=1.0/math.sqrt(GX*GY*GZ)
    out=np.zeros((16,16,256),BF)
    fx=np.arange(64)
    for d in range(16):
        xs=4*d+np.arange(4)
        ang=2*np.pi/GX*((fx[None,:]*xs[:,None])%GX)
        c=np.cos(ang)*factor; s=np.sin(ang)*factor
        for f,sig in ((0,1.0),(1,-1.0)):
            t=np.concatenate([c,sig*s,sig*c,-s],axis=0)
            hi,lo=split_hi_lo(t)
            out[d,:,f*64:(f+1)*64]=hi; out[d,:,128+f*64:128+(f+1)*64]=lo
    return out

def fft8(v):
    def add(a,b): return (a[0]+b[0],a[1]+b[1])
    def sub(a,b): return (a[0]-b[0],a[1]-b[1])
    def mi(a): return (a[1],-a[0])
    r=np.float32(math.sqrt(0.5))
    def fft4(x0,x1,x2,x3):
        a=add(x0,x2); b=sub(x0,x2); c=add(x1,x3); d=mi(sub(x1,x3))
        return add(a,c),add(b,d),sub(a,c),sub(b,d)
    e=fft4(v[0],v[2],v[4],v[6]); o=fft4(v[1],v[3],v[5],v[7])
    o1=((o[1][0]+o[1][1])*r,(o[1][1]-o[1][0])*r)
    o2=mi(o[2])
    o3=((o[3][1]-o[3][0])*r,-(o[3][0]+o[3][1])*r)
    os=(o[0],o1,o2,o3)
    return [add(e[k],os[k]) for k in range(4)]+[sub(e[k],os[k]) for k in range(4)]

def transform_kernel(val_s, con_s, ev_s, ec_s, pv, pc, gmap, ztab, xtabs, out, wout, rho, Z, Z2, GA, GB, xtab, rows_v, kcode, row_s, xsem, rsem):
    step=pl.program_id(0)
    place=lax.axis_index("row")*4+lax.axis_index("col")
    fetch=pltpu.make_async_copy(xtabs.at[place],xtab,xsem)
    move=pltpu.make_async_copy(rows_v,row_s,rsem)
    @pl.when(step==0)
    def _():
        fetch.start()
        g=gmap[...]
        q=((g.astype(jnp.float32)+0.5)*np.float32(1.0/GZ)).astype(jnp.int32)
        fz=g-q*GZ; fy=q&63; fx=q>>6
        flip=fz>96
        fz=jnp.where(flip,GZ-fz,fz)
        fy=jnp.where(flip,(64-fy)&63,fy)
        rows_v[...]=((fy&7)*8+(fy>>3))*(2*KZ)+2*fz
        kcode[...]=jnp.where(flip,64,0)+fx
        move.start()
        first=lax.axis_index("row")*8
        pid=lax.broadcasted_iota(jnp.int32,(16,128),0)%8
        ev=jnp.zeros((16,128),jnp.float32); ec=jnp.ones((16,128),jnp.float32)
        for p in range(8):
            ev=jnp.where(pid==p,ev_s[val_s[first+p]],ev)
            ec=jnp.where(pid==p,ec_s[con_s[first+p]],ec)
        wout[...]=-2.0/(math.sqrt(512)*(ec-ev))
    sub=lax.broadcasted_iota(jnp.int32,(64,96),0); lane=lax.broadcasted_iota(jnp.int32,(64,96),1)
    want=jnp.zeros((64,96),jnp.int32)
    for p in range(32):
        want=jnp.where(sub==p, val_s[p], want)
        want=jnp.where(sub==32+p, con_s[p]+32, want)
    sel=(want==lane).astype(jnp.bfloat16)
    CH=512
    for u in range(12288//CH):
        o=u*CH
        src=jnp.concatenate([pv[:,o:o+CH],pc[:,o:o+CH]],axis=0)
        res=jnp.dot(sel,src,preferred_element_type=jnp.float32)
        rho[step,:,o:o+CH]=(res[:32]*res[32:]).astype(jnp.bfloat16)

    @pl.when(step==3)
    def _():
        fetch.wait()
        move.wait()
        for b in range(8):
            wt=ztab[b%2]
            for ah in range(4):
                parts=[]
                for a in (2*ah,2*ah+1):
                    yp=4*a+b//2; o=384*yp+128*(b%2)
                    for x in range(4):
                        parts.append(rho[x,:,o:o+256])
                B=jnp.concatenate(parts,axis=0)
                B=jnp.concatenate([B,B],axis=1)
                res=lax.dot_general(wt,B,(((1,),(1,)),((),())),preferred_element_type=jnp.float32)
                Z[pl.ds((8*(2*ah)+b)*2*KZ,2*KZ),:]=res[:,:128]
                Z[pl.ds((8*(2*ah+1)+b)*2*KZ,2*KZ),:]=res[:,128:]
        tw=[[np.exp(-2j*np.pi*b*k/64) for k in range(8)] for b in range(8)]
        def pass1(j,_):
            r0=pl.multiple_of(j*8,8)
            for b in range(8):
                v=[(Z[pl.ds((8*a+b)*2*KZ+r0,8),:],Z[pl.ds((8*a+b)*2*KZ+KZ+r0,8),:]) for a in range(8)]
                w=fft8(v)
                for k in range(8):
                    re,im=w[k]
                    if b and k:
                        c=np.float32(tw[b][k].real); s=np.float32(tw[b][k].imag)
                        re,im=re*c-im*s, re*s+im*c
                    Z[pl.ds((8*k+b)*2*KZ+r0,8),:]=re; Z[pl.ds((8*k+b)*2*KZ+KZ+r0,8),:]=im
            return 0
        lax.fori_loop(0,KZ//8,pass1,0)
        def pass2(j,_):
            r0=pl.multiple_of(j*8,8)
            for k1 in range(8):
                v=[(Z[pl.ds((8*k1+b)*2*KZ+r0,8),:],Z[pl.ds((8*k1+b)*2*KZ+KZ+r0,8),:]) for b in range(8)]
                w=fft8(v)
                for k in range(8):
                    re,im=w[k]
                    base=(8*k1+k)*2*KZ+2*r0
                    Z2[pl.ds(base,8,stride=2),:]=re; Z2[pl.ds(base+1,8,stride=2),:]=im
            return 0
        lax.fori_loop(0,KZ//8,pass2,0)
        ksub=lax.broadcasted_iota(jnp.int32,(128,128),0)
        def gather(t,G):
            for j in range(256):
                rr=pl.multiple_of(row_s[2*t+j//128,j%128],2)
                G[pl.ds(2*j,2),:]=Z2[pl.ds(rr,2),:]
        def phase(t,G):
            c=t//4
            for h in range(2):
                oh=(ksub==kcode[pl.ds(2*t+h,1),:]).astype(jnp.bfloat16)
                oh=jnp.concatenate([oh,oh],axis=0)
                co=jnp.dot(xtab[...],oh,preferred_element_type=jnp.float32)
                R=G[pl.ds(256*h,128,stride=2),:].T; I=G[pl.ds(256*h+1,128,stride=2),:].T
                re=0.0; im=0.0
                for x in range(4):
                    rx=R[32*x:32*x+32]; ix=I[32*x:32*x+32]
                    re=re+co[x:x+1]*rx+co[4+x:5+x]*ix
                    im=im+co[8+x:9+x]*ix+co[12+x:13+x]*rx
                at=pl.multiple_of((t%4)*256+h*128,128)
                for r in range(4):
                    both=jnp.concatenate([re[8*r:8*r+8],im[8*r:8*r+8]],axis=0)
                    out[r*4+c,:,pl.ds(at,128)]=both.astype(jnp.bfloat16)
        gather(0,GA)
        def pairs(u,_):
            t=2*u
            gather(t+1,GB); phase(t,GA)
            gather(jnp.minimum(t+2,15),GA); phase(t+1,GB)
            return 0
        lax.fori_loop(0,8,pairs,0)

def partial_transform(val_idx,con_idx,e_val,e_con,pv,pc,gmap):
    smem=pl.BlockSpec(memory_space=pltpu.SMEM)
    return pl.pallas_call(
        transform_kernel,
        grid=(4,),
        in_specs=[smem,smem,smem,smem,
                  pl.BlockSpec((32,12288),lambda i:(0,i)),
                  pl.BlockSpec((64,12288),lambda i:(0,i)),
                  pl.BlockSpec((32,128),lambda i:(0,0)),
                  pl.BlockSpec((2,2*KZ,512),lambda i:(0,0,0)),
                  pl.BlockSpec(memory_space=pl.ANY)],
        out_specs=[pl.BlockSpec((16,16,1024),lambda i:(0,0,0)),pl.BlockSpec((16,128),lambda i:(0,0))],
        scratch_shapes=[pltpu.VMEM((4,32,12288),jnp.bfloat16),
                        pltpu.VMEM((64*2*KZ,128),jnp.float32),
                        pltpu.VMEM((64*2*KZ,128),jnp.float32),
                        pltpu.VMEM((512,128),jnp.float32),
                        pltpu.VMEM((512,128),jnp.float32),
                        pltpu.VMEM((16,256),jnp.bfloat16),
                        pltpu.VMEM((32,128),jnp.int32),
                        pltpu.VMEM((32,128),jnp.int32),
                        pltpu.SMEM((32,128),jnp.int32),
                        pltpu.SemaphoreType.DMA,
                        pltpu.SemaphoreType.DMA],
        out_shape=[jax.ShapeDtypeStruct((16,16,1024),jnp.bfloat16),jax.ShapeDtypeStruct((16,128),jnp.float32)],
        compiler_params=pltpu.CompilerParams(vmem_limit_bytes=60*2**20, dimension_semantics=("arbitrary",)),
        name="partial_transform",
    )(val_idx,con_idx,e_val,e_con,pv,pc,gmap.reshape(32,128),jnp.asarray(z_tables()),jnp.asarray(x_tables()))

def body(psi_val, psi_con, e_val, e_con, val_idx, con_idx, gmap):
    part,w=partial_transform(val_idx,con_idx,e_val,e_con,psi_val,psi_con,gmap)
    recv=lax.all_to_all(part,("row","col"),split_axis=0,concat_axis=0,tiled=True)
    own=recv.astype(jnp.float32).sum(0).astype(jnp.bfloat16)
    every=lax.all_gather(own,"col",axis=0)
    weighted=(every.astype(jnp.float32)*w[None,:,:1]).astype(jnp.bfloat16)
    rowside=weighted.reshape(4,16,2,512).transpose(0,2,1,3).reshape(8,1,16,512)
    colside=own.reshape(16,2,512).transpose(1,0,2).reshape(1,2,16,512)
    payload=jnp.concatenate([jnp.broadcast_to(colside,(8,2,16,512)),jnp.broadcast_to(rowside,(8,2,16,512))],axis=3).reshape(16,16,1024)
    groups=lax.all_to_all(payload,("ph","pl"),split_axis=0,concat_axis=0,tiled=True).reshape(256,1024)
    tiles=lax.dot_general(groups[:,512:],groups[:,:512],(((0,),(0,)),((),())),preferred_element_type=jnp.float32).astype(jnp.bfloat16)
    tiles=lax.all_to_all(tiles.reshape(8,64,512),("pl","row"),split_axis=0,concat_axis=0,tiled=True)
    sums=tiles.reshape(2,4,64,512).astype(jnp.float32).sum(1)
    return jnp.concatenate([sums[0],sums[1]],axis=1)

def solution(mesh):
    fine=Mesh(mesh.devices.reshape(8,2,4,4),("ph","pl","row","col"))
    pair=("ph","pl")
    return jax.shard_map(
        body,
        mesh=fine,
        in_specs=(
            P(None, ("row", "col")),
            P(None, ("row", "col")),
            P(),
            P(),
            P(pair),
            P(pair),
            P(),
        ),
        out_specs=P(("ph","pl","row"), "col"),
        check_vma=False,
    )
```

```python
import math
import numpy as np
import jax, jax.numpy as jnp
from jax import lax
from jax.experimental import pallas as pl
from jax.experimental.pallas import tpu as pltpu
from jax.sharding import Mesh, PartitionSpec as P
import ml_dtypes
BF=ml_dtypes.bfloat16
GX=64;GY=64;GZ=192;NG=4096
KZ=104

def split_hi_lo(t):
    hi=t.astype(np.float32).astype(BF); lo=(t-hi.astype(np.float64)).astype(np.float32).astype(BF)
    return hi,lo

def z_tables():
    z=np.arange(GZ); k=np.arange(97)
    ang=2*np.pi/GZ*((k[:,None]*z[None,:])%GZ)
    t=np.zeros((2,KZ,GZ)); t[0,:97]=np.cos(ang); t[1,:97]=-np.sin(ang)
    t=t.reshape(2*KZ,GZ)
    out=np.zeros((2,2*KZ,512),BF)
    hi,lo=split_hi_lo(t)
    for par,off in ((0,0),(1,64)):
        out[par,:,off:off+GZ]=hi; out[par,:,256+off:256+off+GZ]=lo
    return out

def x_tables():
    factor=1.0/math.sqrt(GX*GY*GZ)
    out=np.zeros((16,16,256),BF)
    fx=np.arange(64)
    for d in range(16):
        xs=4*d+np.arange(4)
        ang=2*np.pi/GX*((fx[None,:]*xs[:,None])%GX)
        c=np.cos(ang)*factor; s=np.sin(ang)*factor
        for f,sig in ((0,1.0),(1,-1.0)):
            t=np.concatenate([c,sig*s,sig*c,-s],axis=0)
            hi,lo=split_hi_lo(t)
            out[d,:,f*64:(f+1)*64]=hi; out[d,:,128+f*64:128+(f+1)*64]=lo
    return out

def fft8(v):
    def add(a,b): return (a[0]+b[0],a[1]+b[1])
    def sub(a,b): return (a[0]-b[0],a[1]-b[1])
    def mi(a): return (a[1],-a[0])
    r=np.float32(math.sqrt(0.5))
    def fft4(x0,x1,x2,x3):
        a=add(x0,x2); b=sub(x0,x2); c=add(x1,x3); d=mi(sub(x1,x3))
        return add(a,c),add(b,d),sub(a,c),sub(b,d)
    e=fft4(v[0],v[2],v[4],v[6]); o=fft4(v[1],v[3],v[5],v[7])
    o1=((o[1][0]+o[1][1])*r,(o[1][1]-o[1][0])*r)
    o2=mi(o[2])
    o3=((o[3][1]-o[3][0])*r,-(o[3][0]+o[3][1])*r)
    os=(o[0],o1,o2,o3)
    return [add(e[k],os[k]) for k in range(4)]+[sub(e[k],os[k]) for k in range(4)]

def transform_kernel(val_s, con_s, ev_s, ec_s, pv, pc, gmap, ztab, xtabs, out, wout, va, vb, rho, Z, Z2, GA, GB, xtab, rows_v, kcode, row_s, asem, bsem, xsem, rsem):
    place=lax.axis_index("row")*4+lax.axis_index("col")
    planes=[(pltpu.make_async_copy(pv.at[:,pl.ds(12288*x,12288)],va.at[x],asem.at[x]),
             pltpu.make_async_copy(pc.at[:,pl.ds(12288*x,12288)],vb.at[x],bsem.at[x])) for x in range(4)]
    for one in planes:
        one[0].start()
        one[1].start()
    fetch=pltpu.make_async_copy(xtabs.at[place],xtab,xsem)
    fetch.start()
    g=gmap[...]
    q=((g.astype(jnp.float32)+0.5)*np.float32(1.0/GZ)).astype(jnp.int32)
    fz=g-q*GZ; fy=q&63; fx=q>>6
    flip=fz>96
    fz=jnp.where(flip,GZ-fz,fz)
    fy=jnp.where(flip,(64-fy)&63,fy)
    rows_v[...]=((fy&7)*8+(fy>>3))*(2*KZ)+2*fz
    kcode[...]=jnp.where(flip,64,0)+fx
    move=pltpu.make_async_copy(rows_v,row_s,rsem)
    move.start()
    first=lax.axis_index("row")*8
    pid=lax.broadcasted_iota(jnp.int32,(16,128),0)%8
    ev=jnp.zeros((16,128),jnp.float32); ec=jnp.ones((16,128),jnp.float32)
    for p in range(8):
        ev=jnp.where(pid==p,ev_s[val_s[first+p]],ev)
        ec=jnp.where(pid==p,ec_s[con_s[first+p]],ec)
    wout[...]=-2.0/(math.sqrt(512)*(ec-ev))
    sub=lax.broadcasted_iota(jnp.int32,(8,96),0); lane=lax.broadcasted_iota(jnp.int32,(8,96),1)
    picks=[]
    for q in range(8):
        want=jnp.zeros((8,96),jnp.int32)
        for k in range(8):
            p=8*q+k
            want=jnp.where(sub==k, val_s[p] if p<32 else con_s[p-32]+32, want)
        picks.append((want==lane).astype(jnp.float32))
    sel=jnp.concatenate(picks,axis=0).astype(jnp.bfloat16)
    CH=512
    for x in range(4):
        planes[x][0].wait()
        planes[x][1].wait()
        for u in range(12288//CH):
            o=u*CH
            src=jnp.concatenate([va[x,:,o:o+CH],vb[x,:,o:o+CH]],axis=0)
            res=jnp.dot(sel,src,preferred_element_type=jnp.float32)
            rho[x,:,o:o+CH]=(res[:32]*res[32:]).astype(jnp.bfloat16)
    fetch.wait()
    move.wait()
    for b in range(8):
        wt=ztab[b%2]
        for ah in range(4):
            parts=[]
            for a in (2*ah,2*ah+1):
                yp=4*a+b//2; o=384*yp+128*(b%2)
                for x in range(4):
                    parts.append(rho[x,:,o:o+256])
            B=jnp.concatenate(parts,axis=0)
            B=jnp.concatenate([B,B],axis=1)
            res=lax.dot_general(wt,B,(((1,),(1,)),((),())),preferred_element_type=jnp.float32)
            Z[pl.ds((8*(2*ah)+b)*2*KZ,2*KZ),:]=res[:,:128]
            Z[pl.ds((8*(2*ah+1)+b)*2*KZ,2*KZ),:]=res[:,128:]
    tw=[[np.exp(-2j*np.pi*b*k/64) for k in range(8)] for b in range(8)]
    def pass1(j,_):
        r0=pl.multiple_of(j*8,8)
        for b in range(8):
            v=[(Z[pl.ds((8*a+b)*2*KZ+r0,8),:],Z[pl.ds((8*a+b)*2*KZ+KZ+r0,8),:]) for a in range(8)]
            w=fft8(v)
            for k in range(8):
                re,im=w[k]
                if b and k:
                    c=np.float32(tw[b][k].real); s=np.float32(tw[b][k].imag)
                    re,im=re*c-im*s, re*s+im*c
                Z[pl.ds((8*k+b)*2*KZ+r0,8),:]=re; Z[pl.ds((8*k+b)*2*KZ+KZ+r0,8),:]=im
        return 0
    lax.fori_loop(0,KZ//8,pass1,0)
    def pass2(j,_):
        r0=pl.multiple_of(j*8,8)
        for k1 in range(8):
            v=[(Z[pl.ds((8*k1+b)*2*KZ+r0,8),:],Z[pl.ds((8*k1+b)*2*KZ+KZ+r0,8),:]) for b in range(8)]
            w=fft8(v)
            for k in range(8):
                re,im=w[k]
                base=(8*k1+k)*2*KZ+2*r0
                Z2[pl.ds(base,8,stride=2),:]=re; Z2[pl.ds(base+1,8,stride=2),:]=im
        return 0
    lax.fori_loop(0,KZ//8,pass2,0)
    ksub=lax.broadcasted_iota(jnp.int32,(128,128),0)
    def gather(t,G):
        for j in range(256):
            rr=pl.multiple_of(row_s[2*t+j//128,j%128],2)
            G[pl.ds(2*j,2),:]=Z2[pl.ds(rr,2),:]
    def phase(t,G):
        c=t//4
        for h in range(2):
            oh=(ksub==kcode[pl.ds(2*t+h,1),:]).astype(jnp.bfloat16)
            oh=jnp.concatenate([oh,oh],axis=0)
            co=jnp.dot(xtab[...],oh,preferred_element_type=jnp.float32)
            R=G[pl.ds(256*h,128,stride=2),:].T; I=G[pl.ds(256*h+1,128,stride=2),:].T
            re=0.0; im=0.0
            for x in range(4):
                rx=R[32*x:32*x+32]; ix=I[32*x:32*x+32]
                re=re+co[x:x+1]*rx+co[4+x:5+x]*ix
                im=im+co[8+x:9+x]*ix+co[12+x:13+x]*rx
            at=pl.multiple_of((t%4)*256+h*128,128)
            for r in range(4):
                both=jnp.concatenate([re[8*r:8*r+8],im[8*r:8*r+8]],axis=0)
                out[r*4+c,:,pl.ds(at,128)]=both.astype(jnp.bfloat16)
    gather(0,GA)
    for t in range(16):
        if t<15:
            gather(t+1,(GA,GB)[(t+1)%2])
        phase(t,(GA,GB)[t%2])

def partial_transform(val_idx,con_idx,e_val,e_con,pv,pc,gmap):
    smem=pl.BlockSpec(memory_space=pltpu.SMEM)
    return pl.pallas_call(
        transform_kernel,
        grid=(1,),
        in_specs=[smem,smem,smem,smem,
                  pl.BlockSpec(memory_space=pl.ANY),
                  pl.BlockSpec(memory_space=pl.ANY),
                  pl.BlockSpec((32,128),lambda i:(0,0)),
                  pl.BlockSpec((2,2*KZ,512),lambda i:(0,0,0)),
                  pl.BlockSpec(memory_space=pl.ANY)],
        out_specs=[pl.BlockSpec((16,16,1024),lambda i:(0,0,0)),pl.BlockSpec((16,128),lambda i:(0,0))],
        scratch_shapes=[pltpu.VMEM((4,32,12288),jnp.bfloat16),
                        pltpu.VMEM((4,64,12288),jnp.bfloat16),
                        pltpu.VMEM((4,32,12288),jnp.bfloat16),
                        pltpu.VMEM((64*2*KZ,128),jnp.float32),
                        pltpu.VMEM((64*2*KZ,128),jnp.float32),
                        pltpu.VMEM((512,128),jnp.float32),
                        pltpu.VMEM((512,128),jnp.float32),
                        pltpu.VMEM((16,256),jnp.bfloat16),
                        pltpu.VMEM((32,128),jnp.int32),
                        pltpu.VMEM((32,128),jnp.int32),
                        pltpu.SMEM((32,128),jnp.int32),
                        pltpu.SemaphoreType.DMA((4,)),
                        pltpu.SemaphoreType.DMA((4,)),
                        pltpu.SemaphoreType.DMA,
                        pltpu.SemaphoreType.DMA],
        out_shape=[jax.ShapeDtypeStruct((16,16,1024),jnp.bfloat16),jax.ShapeDtypeStruct((16,128),jnp.float32)],
        compiler_params=pltpu.CompilerParams(vmem_limit_bytes=60*2**20, dimension_semantics=("arbitrary",)),
        name="partial_transform",
    )(val_idx,con_idx,e_val,e_con,pv,pc,gmap.reshape(32,128),jnp.asarray(z_tables()),jnp.asarray(x_tables()))

def body(psi_val, psi_con, e_val, e_con, val_idx, con_idx, gmap):
    part,w=partial_transform(val_idx,con_idx,e_val,e_con,psi_val,psi_con,gmap)
    recv=lax.all_to_all(part,("row","col"),split_axis=0,concat_axis=0,tiled=True)
    own=recv.astype(jnp.float32).sum(0).astype(jnp.bfloat16)
    every=lax.all_gather(own,"col",axis=0)
    weighted=(every.astype(jnp.float32)*w[None,:,:1]).astype(jnp.bfloat16)
    rowside=weighted.reshape(4,16,2,512).transpose(0,2,1,3).reshape(8,1,16,512)
    colside=own.reshape(16,2,512).transpose(1,0,2).reshape(1,2,16,512)
    payload=jnp.concatenate([jnp.broadcast_to(colside,(8,2,16,512)),jnp.broadcast_to(rowside,(8,2,16,512))],axis=3).reshape(16,16,1024)
    groups=lax.all_to_all(payload,("ph","pl"),split_axis=0,concat_axis=0,tiled=True).reshape(256,1024)
    tiles=lax.dot_general(groups[:,512:],groups[:,:512],(((0,),(0,)),((),())),preferred_element_type=jnp.float32).astype(jnp.bfloat16)
    tiles=lax.all_to_all(tiles.reshape(8,64,512),("pl","row"),split_axis=0,concat_axis=0,tiled=True)
    sums=tiles.reshape(2,4,64,512).astype(jnp.float32).sum(1)
    return jnp.concatenate([sums[0],sums[1]],axis=1)

def solution(mesh):
    fine=Mesh(mesh.devices.reshape(8,2,4,4),("ph","pl","row","col"))
    pair=("ph","pl")
    return jax.shard_map(
        body,
        mesh=fine,
        in_specs=(
            P(None, ("row", "col")),
            P(None, ("row", "col")),
            P(),
            P(),
            P(pair),
            P(pair),
            P(),
        ),
        out_specs=P(("ph","pl","row"), "col"),
        check_vma=False,
    )
```

```python
import math
import numpy as np
import jax, jax.numpy as jnp
from jax import lax
from jax.experimental import pallas as pl
from jax.experimental.pallas import tpu as pltpu
from jax.sharding import Mesh, PartitionSpec as P
import ml_dtypes
BF=ml_dtypes.bfloat16
GX=64;GY=64;GZ=192;NG=4096
KZ=104

def split_hi_lo(t):
    hi=t.astype(np.float32).astype(BF); lo=(t-hi.astype(np.float64)).astype(np.float32).astype(BF)
    return hi,lo

def z_tables():
    z=np.arange(GZ); k=np.arange(97)
    ang=2*np.pi/GZ*((k[:,None]*z[None,:])%GZ)
    t=np.zeros((2,KZ,GZ)); t[0,:97]=np.cos(ang); t[1,:97]=-np.sin(ang)
    t=t.reshape(2*KZ,GZ)
    out=np.zeros((2,4*KZ,256),BF)
    hi,lo=split_hi_lo(t)
    for par,off in ((0,0),(1,64)):
        out[par,:2*KZ,off:off+GZ]=hi; out[par,2*KZ:,off:off+GZ]=lo
    return out

def x_tables():
    factor=1.0/math.sqrt(GX*GY*GZ)
    out=np.zeros((16,16,256),BF)
    fx=np.arange(64)
    for d in range(16):
        xs=4*d+np.arange(4)
        ang=2*np.pi/GX*((fx[None,:]*xs[:,None])%GX)
        c=np.cos(ang)*factor; s=np.sin(ang)*factor
        for f,sig in ((0,1.0),(1,-1.0)):
            t=np.concatenate([c,sig*s,sig*c,-s],axis=0)
            hi,lo=split_hi_lo(t)
            out[d,:,f*64:(f+1)*64]=hi; out[d,:,128+f*64:128+(f+1)*64]=lo
    return out

def fft8(v):
    def add(a,b): return (a[0]+b[0],a[1]+b[1])
    def sub(a,b): return (a[0]-b[0],a[1]-b[1])
    def mi(a): return (a[1],-a[0])
    r=np.float32(math.sqrt(0.5))
    def fft4(x0,x1,x2,x3):
        a=add(x0,x2); b=sub(x0,x2); c=add(x1,x3); d=mi(sub(x1,x3))
        return add(a,c),add(b,d),sub(a,c),sub(b,d)
    e=fft4(v[0],v[2],v[4],v[6]); o=fft4(v[1],v[3],v[5],v[7])
    o1=((o[1][0]+o[1][1])*r,(o[1][1]-o[1][0])*r)
    o2=mi(o[2])
    o3=((o[3][1]-o[3][0])*r,-(o[3][0]+o[3][1])*r)
    os=(o[0],o1,o2,o3)
    return [add(e[k],os[k]) for k in range(4)]+[sub(e[k],os[k]) for k in range(4)]

def transform_kernel(val_s, con_s, ev_s, ec_s, pv, pc, gmap, ztab, xtabs, out, wout, va, vb, rho, Z, Z2, GA, GB, xtab, rows_v, kcode, row_s, asem, bsem, xsem, rsem):
    place=lax.axis_index("row")*4+lax.axis_index("col")
    planes=[(pltpu.make_async_copy(pv.at[:,pl.ds(12288*x,12288)],va.at[x],asem.at[x]),
             pltpu.make_async_copy(pc.at[:,pl.ds(12288*x,12288)],vb.at[x],bsem.at[x])) for x in range(4)]
    for one in planes:
        one[0].start()
        one[1].start()
    fetch=pltpu.make_async_copy(xtabs.at[place],xtab,xsem)
    fetch.start()
    g=gmap[...]
    q=((g.astype(jnp.float32)+0.5)*np.float32(1.0/GZ)).astype(jnp.int32)
    fz=g-q*GZ; fy=q&63; fx=q>>6
    flip=fz>96
    fz=jnp.where(flip,GZ-fz,fz)
    fy=jnp.where(flip,(64-fy)&63,fy)
    rows_v[...]=((fy&7)*8+(fy>>3))*(2*KZ)+2*fz
    kcode[...]=jnp.where(flip,64,0)+fx
    move=pltpu.make_async_copy(rows_v,row_s,rsem)
    move.start()
    first=lax.axis_index("row")*8
    pid=lax.broadcasted_iota(jnp.int32,(16,128),0)%8
    ev=jnp.zeros((16,128),jnp.float32); ec=jnp.ones((16,128),jnp.float32)
    for p in range(8):
        ev=jnp.where(pid==p,ev_s[val_s[first+p]],ev)
        ec=jnp.where(pid==p,ec_s[con_s[first+p]],ec)
    wout[...]=-2.0/(math.sqrt(512)*(ec-ev))
    sub=lax.broadcasted_iota(jnp.int32,(8,96),0); lane=lax.broadcasted_iota(jnp.int32,(8,96),1)
    picks=[]
    for q in range(8):
        want=jnp.zeros((8,96),jnp.int32)
        for k in range(8):
            p=8*q+k
            want=jnp.where(sub==k, val_s[p] if p<32 else con_s[p-32]+32, want)
        picks.append((want==lane).astype(jnp.float32))
    sel=jnp.concatenate(picks,axis=0).astype(jnp.bfloat16)
    CH=512
    for x in range(4):
        planes[x][0].wait()
        planes[x][1].wait()
        for u in range(12288//CH):
            o=u*CH
            src=jnp.concatenate([va[x,:,o:o+CH],vb[x,:,o:o+CH]],axis=0)
            res=jnp.dot(sel,src,preferred_element_type=jnp.float32)
            rho[x,:,o:o+CH]=(res[:32]*res[32:]).astype(jnp.bfloat16)
    fetch.wait()
    move.wait()
    for b in range(8):
        wt=ztab[b%2]
        for ah in range(0,8,2):
            parts=[]
            for a in range(ah,ah+2):
                o=384*(4*a+b//2)+128*(b%2)
                for x in range(4):
                    parts.append(rho[x,:,o:o+256])
            B=jnp.concatenate(parts,axis=0)
            res=lax.dot_general(wt,B,(((1,),(1,)),((),())),preferred_element_type=jnp.float32)
            res=res[:2*KZ]+res[2*KZ:]
            for a in range(2):
                Z[pl.ds((8*(ah+a)+b)*2*KZ,2*KZ),:]=res[:,128*a:128*a+128]
    tw=[[np.exp(-2j*np.pi*b*k/64) for k in range(8)] for b in range(8)]
    def pass1(j,_):
        r0=pl.multiple_of(j*8,8)
        for b in range(8):
            v=[(Z[pl.ds((8*a+b)*2*KZ+r0,8),:],Z[pl.ds((8*a+b)*2*KZ+KZ+r0,8),:]) for a in range(8)]
            w=fft8(v)
            for k in range(8):
                re,im=w[k]
                if b and k:
                    c=np.float32(tw[b][k].real); s=np.float32(tw[b][k].imag)
                    re,im=re*c-im*s, re*s+im*c
                Z[pl.ds((8*k+b)*2*KZ+r0,8),:]=re; Z[pl.ds((8*k+b)*2*KZ+KZ+r0,8),:]=im
        return 0
    lax.fori_loop(0,KZ//8,pass1,0,unroll=True)
    def pass2(j,_):
        r0=pl.multiple_of(j*8,8)
        for k1 in range(8):
            v=[(Z[pl.ds((8*k1+b)*2*KZ+r0,8),:],Z[pl.ds((8*k1+b)*2*KZ+KZ+r0,8),:]) for b in range(8)]
            w=fft8(v)
            for k in range(8):
                re,im=w[k]
                base=(8*k1+k)*2*KZ+2*r0
                Z2[pl.ds(base,8,stride=2),:]=re; Z2[pl.ds(base+1,8,stride=2),:]=im
        return 0
    lax.fori_loop(0,KZ//8,pass2,0)
    ksub=lax.broadcasted_iota(jnp.int32,(128,128),0)
    def gather(t,G):
        for j in range(256):
            rr=pl.multiple_of(row_s[2*t+j//128,j%128],2)
            G[pl.ds(2*j,2),:]=Z2[pl.ds(rr,2),:]
    def phase(t,G):
        c=t//4
        for h in range(2):
            oh=(ksub==kcode[pl.ds(2*t+h,1),:]).astype(jnp.bfloat16)
            oh=jnp.concatenate([oh,oh],axis=0)
            co=jnp.dot(xtab[...],oh,preferred_element_type=jnp.float32)
            R=G[pl.ds(256*h,128,stride=2),:].T; I=G[pl.ds(256*h+1,128,stride=2),:].T
            re=0.0; im=0.0
            for x in range(4):
                rx=R[32*x:32*x+32]; ix=I[32*x:32*x+32]
                re=re+co[x:x+1]*rx+co[4+x:5+x]*ix
                im=im+co[8+x:9+x]*ix+co[12+x:13+x]*rx
            at=pl.multiple_of((t%4)*256+h*128,128)
            for r in range(4):
                both=jnp.concatenate([re[8*r:8*r+8],im[8*r:8*r+8]],axis=0)
                out[r*4+c,:,pl.ds(at,128)]=both.astype(jnp.bfloat16)
    gather(0,GA)
    for t in range(16):
        if t<15:
            gather(t+1,(GA,GB)[(t+1)%2])
        phase(t,(GA,GB)[t%2])

def partial_transform(val_idx,con_idx,e_val,e_con,pv,pc,gmap):
    smem=pl.BlockSpec(memory_space=pltpu.SMEM)
    return pl.pallas_call(
        transform_kernel,
        grid=(1,),
        in_specs=[smem,smem,smem,smem,
                  pl.BlockSpec(memory_space=pl.ANY),
                  pl.BlockSpec(memory_space=pl.ANY),
                  pl.BlockSpec((32,128),lambda i:(0,0)),
                  pl.BlockSpec((2,4*KZ,256),lambda i:(0,0,0)),
                  pl.BlockSpec(memory_space=pl.ANY)],
        out_specs=[pl.BlockSpec((16,16,1024),lambda i:(0,0,0)),pl.BlockSpec((16,128),lambda i:(0,0))],
        scratch_shapes=[pltpu.VMEM((4,32,12288),jnp.bfloat16),
                        pltpu.VMEM((4,64,12288),jnp.bfloat16),
                        pltpu.VMEM((4,32,12288),jnp.bfloat16),
                        pltpu.VMEM((64*2*KZ,128),jnp.float32),
                        pltpu.VMEM((64*2*KZ,128),jnp.float32),
                        pltpu.VMEM((512,128),jnp.float32),
                        pltpu.VMEM((512,128),jnp.float32),
                        pltpu.VMEM((16,256),jnp.bfloat16),
                        pltpu.VMEM((32,128),jnp.int32),
                        pltpu.VMEM((32,128),jnp.int32),
                        pltpu.SMEM((32,128),jnp.int32),
                        pltpu.SemaphoreType.DMA((4,)),
                        pltpu.SemaphoreType.DMA((4,)),
                        pltpu.SemaphoreType.DMA,
                        pltpu.SemaphoreType.DMA],
        out_shape=[jax.ShapeDtypeStruct((16,16,1024),jnp.bfloat16),jax.ShapeDtypeStruct((16,128),jnp.float32)],
        compiler_params=pltpu.CompilerParams(vmem_limit_bytes=60*2**20, dimension_semantics=("arbitrary",)),
        name="partial_transform",
    )(val_idx,con_idx,e_val,e_con,pv,pc,gmap.reshape(32,128),jnp.asarray(z_tables()),jnp.asarray(x_tables()))

def body(psi_val, psi_con, e_val, e_con, val_idx, con_idx, gmap):
    part,w=partial_transform(val_idx,con_idx,e_val,e_con,psi_val,psi_con,gmap)
    recv=lax.all_to_all(part,("row","col"),split_axis=0,concat_axis=0,tiled=True)
    own=recv.astype(jnp.float32).sum(0).astype(jnp.bfloat16)
    every=lax.all_gather(own,"col",axis=0)
    weighted=(every.astype(jnp.float32)*w[None,:,:1]).astype(jnp.bfloat16)
    rowside=weighted.reshape(4,16,2,512).transpose(0,2,1,3).reshape(8,1,16,512)
    colside=own.reshape(16,2,512).transpose(1,0,2).reshape(1,2,16,512)
    payload=jnp.concatenate([jnp.broadcast_to(colside,(8,2,16,512)),jnp.broadcast_to(rowside,(8,2,16,512))],axis=3).reshape(16,16,1024)
    groups=lax.all_to_all(payload,("ph","pl"),split_axis=0,concat_axis=0,tiled=True).reshape(256,1024)
    tiles=lax.dot_general(groups[:,512:],groups[:,:512],(((0,),(0,)),((),())),preferred_element_type=jnp.float32).astype(jnp.bfloat16)
    tiles=lax.all_to_all(tiles.reshape(8,64,512),("pl","row"),split_axis=0,concat_axis=0,tiled=True)
    sums=tiles.reshape(2,4,64,512).astype(jnp.float32).sum(1)
    return jnp.concatenate([sums[0],sums[1]],axis=1)

def solution(mesh):
    fine=Mesh(mesh.devices.reshape(8,2,4,4),("ph","pl","row","col"))
    pair=("ph","pl")
    return jax.shard_map(
        body,
        mesh=fine,
        in_specs=(
            P(None, ("row", "col")),
            P(None, ("row", "col")),
            P(),
            P(),
            P(pair),
            P(pair),
            P(),
        ),
        out_specs=P(("ph","pl","row"), "col"),
        check_vma=False,
    )
```

```python
import math
import numpy as np
import jax, jax.numpy as jnp
from jax import lax
from jax.experimental import pallas as pl
from jax.experimental.pallas import tpu as pltpu
from jax.sharding import Mesh, PartitionSpec as P
import ml_dtypes
BF=ml_dtypes.bfloat16
GX=64;GY=64;GZ=192;NG=4096
KZ=104

def split_hi_lo(t):
    hi=t.astype(np.float32).astype(BF); lo=(t-hi.astype(np.float64)).astype(np.float32).astype(BF)
    return hi,lo

def z_tables():
    z=np.arange(GZ); k=np.arange(97)
    ang=2*np.pi/GZ*((k[:,None]*z[None,:])%GZ)
    t=np.zeros((2,KZ,GZ)); t[0,:97]=np.cos(ang); t[1,:97]=-np.sin(ang)
    t=t.reshape(2*KZ,GZ)
    out=np.zeros((2,4*KZ,256),BF)
    hi,lo=split_hi_lo(t)
    for par,off in ((0,0),(1,64)):
        out[par,:2*KZ,off:off+GZ]=hi; out[par,2*KZ:,off:off+GZ]=lo
    return out

def x_tables():
    factor=1.0/math.sqrt(GX*GY*GZ)
    out=np.zeros((16,16,256),BF)
    fx=np.arange(64)
    for d in range(16):
        xs=4*d+np.arange(4)
        ang=2*np.pi/GX*((fx[None,:]*xs[:,None])%GX)
        c=np.cos(ang)*factor; s=np.sin(ang)*factor
        for f,sig in ((0,1.0),(1,-1.0)):
            t=np.concatenate([c,sig*s,sig*c,-s],axis=0)
            hi,lo=split_hi_lo(t)
            out[d,:,f*64:(f+1)*64]=hi; out[d,:,128+f*64:128+(f+1)*64]=lo
    return out

def fft8(v):
    def add(a,b): return (a[0]+b[0],a[1]+b[1])
    def sub(a,b): return (a[0]-b[0],a[1]-b[1])
    def addmi(a,b): return (a[0]+b[1],a[1]-b[0])
    def submi(a,b): return (a[0]-b[1],a[1]+b[0])
    r=np.float32(math.sqrt(0.5))
    def fft4(x0,x1,x2,x3):
        a=add(x0,x2); b=sub(x0,x2); c=add(x1,x3); d=sub(x1,x3)
        return add(a,c),addmi(b,d),sub(a,c),submi(b,d)
    e=fft4(v[0],v[2],v[4],v[6]); o=fft4(v[1],v[3],v[5],v[7])
    o1=((o[1][0]+o[1][1])*r,(o[1][1]-o[1][0])*r)
    o3=((o[3][1]-o[3][0])*r,(o[3][0]+o[3][1])*(-r))
    return [add(e[0],o[0]),add(e[1],o1),addmi(e[2],o[2]),add(e[3],o3),
            sub(e[0],o[0]),sub(e[1],o1),submi(e[2],o[2]),sub(e[3],o3)]

def transform_kernel(val_s, con_s, ev_s, ec_s, pv, pc, gmap, ztabs, xtabs, out, wout, va, vb, ztab, rho, Z, Z2, GA, GB, xtab, rows_v, kcode, row_s, asem, bsem, zsem, xsem, rsem):
    place=lax.axis_index("row")*4+lax.axis_index("col")
    planes=[(pltpu.make_async_copy(pv.at[:,pl.ds(12288*x,12288)],va.at[x],asem.at[x]),
             pltpu.make_async_copy(pc.at[:,pl.ds(12288*x,12288)],vb.at[x],bsem.at[x])) for x in range(4)]
    for one in planes:
        one[0].start()
        one[1].start()
    fetch=pltpu.make_async_copy(xtabs.at[place],xtab,xsem)
    fetch.start()
    table=pltpu.make_async_copy(ztabs,ztab,zsem)
    table.start()
    g=gmap[...]
    q=((g.astype(jnp.float32)+0.5)*np.float32(1.0/GZ)).astype(jnp.int32)
    fz=g-q*GZ; fy=q&63; fx=q>>6
    flip=fz>96
    fz=jnp.where(flip,GZ-fz,fz)
    fy=jnp.where(flip,(64-fy)&63,fy)
    rows_v[...]=((fy&7)*8+(fy>>3))*(2*KZ)+2*fz
    kcode[...]=jnp.where(flip,64,0)+fx
    move=pltpu.make_async_copy(rows_v,row_s,rsem)
    move.start()
    first=lax.axis_index("row")*8
    pid=lax.broadcasted_iota(jnp.int32,(16,128),0)%8
    ev=jnp.zeros((16,128),jnp.float32); ec=jnp.ones((16,128),jnp.float32)
    for p in range(8):
        ev=jnp.where(pid==p,ev_s[val_s[first+p]],ev)
        ec=jnp.where(pid==p,ec_s[con_s[first+p]],ec)
    wout[...]=-2.0/(math.sqrt(512)*(ec-ev))
    sub=lax.broadcasted_iota(jnp.int32,(8,96),0); lane=lax.broadcasted_iota(jnp.int32,(8,96),1)
    picks=[]
    for q in range(8):
        want=jnp.zeros((8,96),jnp.int32)
        for k in range(8):
            p=8*q+k
            want=jnp.where(sub==k, val_s[p] if p<32 else con_s[p-32]+32, want)
        picks.append((want==lane).astype(jnp.float32))
    sel=jnp.concatenate(picks,axis=0).astype(jnp.bfloat16)
    CH=512
    for x in range(4):
        planes[x][0].wait()
        planes[x][1].wait()
        for u in range(12288//CH):
            o=u*CH
            src=jnp.concatenate([va[x,:,o:o+CH],vb[x,:,o:o+CH]],axis=0)
            res=jnp.dot(sel,src,preferred_element_type=jnp.float32)
            rho[x,:,o:o+CH]=(res[:32]*res[32:]).astype(jnp.bfloat16)
    fetch.wait()
    table.wait()
    move.wait()
    for b in range(8):
        wt=ztab[b%2]
        for ah in range(0,8,2):
            parts=[]
            for a in range(ah,ah+2):
                o=384*(4*a+b//2)+128*(b%2)
                for x in range(4):
                    parts.append(rho[x,:,o:o+256])
            B=jnp.concatenate(parts,axis=0)
            res=lax.dot_general(wt,B,(((1,),(1,)),((),())),preferred_element_type=jnp.float32)
            res=res[:2*KZ]+res[2*KZ:]
            for a in range(2):
                Z[pl.ds((8*(ah+a)+b)*2*KZ,2*KZ),:]=res[:,128*a:128*a+128]
    tw=[[np.exp(-2j*np.pi*b*k/64) for k in range(8)] for b in range(8)]
    def pass1(j,_):
        r0=pl.multiple_of(j*8,8)
        for b in range(8):
            v=[(Z[pl.ds((8*a+b)*2*KZ+r0,8),:],Z[pl.ds((8*a+b)*2*KZ+KZ+r0,8),:]) for a in range(8)]
            w=fft8(v)
            for k in range(8):
                re,im=w[k]
                if b and k:
                    c=np.float32(tw[b][k].real); s=np.float32(tw[b][k].imag)
                    re,im=re*c-im*s, re*s+im*c
                Z[pl.ds((8*k+b)*2*KZ+r0,8),:]=re; Z[pl.ds((8*k+b)*2*KZ+KZ+r0,8),:]=im
        return 0
    lax.fori_loop(0,KZ//8,pass1,0,unroll=True)
    def pass2(j,_):
        r0=pl.multiple_of(j*8,8)
        for k1 in range(8):
            v=[(Z[pl.ds((8*k1+b)*2*KZ+r0,8),:],Z[pl.ds((8*k1+b)*2*KZ+KZ+r0,8),:]) for b in range(8)]
            w=fft8(v)
            for k in range(8):
                re,im=w[k]
                base=(8*k1+k)*2*KZ+2*r0
                Z2[pl.ds(base,8,stride=2),:]=re; Z2[pl.ds(base+1,8,stride=2),:]=im
        return 0
    lax.fori_loop(0,KZ//8,pass2,0)
    ksub=lax.broadcasted_iota(jnp.int32,(128,128),0)
    def gather(t,G):
        for j in range(256):
            rr=pl.multiple_of(row_s[2*t+j//128,j%128],2)
            G[pl.ds(2*j,2),:]=Z2[pl.ds(rr,2),:]
    def phase(t,G):
        c=t//4
        for h in range(2):
            oh=(ksub==kcode[pl.ds(2*t+h,1),:]).astype(jnp.bfloat16)
            oh=jnp.concatenate([oh,oh],axis=0)
            co=jnp.dot(xtab[...],oh,preferred_element_type=jnp.float32)
            R=G[pl.ds(256*h,128,stride=2),:].T; I=G[pl.ds(256*h+1,128,stride=2),:].T
            re=0.0; im=0.0
            for x in range(4):
                rx=R[32*x:32*x+32]; ix=I[32*x:32*x+32]
                re=re+co[x:x+1]*rx+co[4+x:5+x]*ix
                im=im+co[8+x:9+x]*ix+co[12+x:13+x]*rx
            at=pl.multiple_of((t%4)*256+h*128,128)
            for r in range(4):
                both=jnp.concatenate([re[8*r:8*r+8],im[8*r:8*r+8]],axis=0)
                out[r*4+c,:,pl.ds(at,128)]=both.astype(jnp.bfloat16)
    gather(0,GA)
    for t in range(16):
        if t<15:
            gather(t+1,(GA,GB)[(t+1)%2])
        phase(t,(GA,GB)[t%2])

def partial_transform(val_idx,con_idx,e_val,e_con,pv,pc,gmap):
    smem=pl.BlockSpec(memory_space=pltpu.SMEM)
    return pl.pallas_call(
        transform_kernel,
        grid=(1,),
        in_specs=[smem,smem,smem,smem,
                  pl.BlockSpec(memory_space=pl.ANY),
                  pl.BlockSpec(memory_space=pl.ANY),
                  pl.BlockSpec((32,128),lambda i:(0,0)),
                  pl.BlockSpec(memory_space=pl.ANY),
                  pl.BlockSpec(memory_space=pl.ANY)],
        out_specs=[pl.BlockSpec((16,16,1024),lambda i:(0,0,0)),pl.BlockSpec((16,128),lambda i:(0,0))],
        scratch_shapes=[pltpu.VMEM((4,32,12288),jnp.bfloat16),
                        pltpu.VMEM((4,64,12288),jnp.bfloat16),
                        pltpu.VMEM((2,4*KZ,256),jnp.bfloat16),
                        pltpu.VMEM((4,32,12288),jnp.bfloat16),
                        pltpu.VMEM((64*2*KZ,128),jnp.float32),
                        pltpu.VMEM((64*2*KZ,128),jnp.float32),
                        pltpu.VMEM((512,128),jnp.float32),
                        pltpu.VMEM((512,128),jnp.float32),
                        pltpu.VMEM((16,256),jnp.bfloat16),
                        pltpu.VMEM((32,128),jnp.int32),
                        pltpu.VMEM((32,128),jnp.int32),
                        pltpu.SMEM((32,128),jnp.int32),
                        pltpu.SemaphoreType.DMA((4,)),
                        pltpu.SemaphoreType.DMA((4,)),
                        pltpu.SemaphoreType.DMA,
                        pltpu.SemaphoreType.DMA,
                        pltpu.SemaphoreType.DMA],
        out_shape=[jax.ShapeDtypeStruct((16,16,1024),jnp.bfloat16),jax.ShapeDtypeStruct((16,128),jnp.float32)],
        compiler_params=pltpu.CompilerParams(vmem_limit_bytes=60*2**20, dimension_semantics=("arbitrary",)),
        name="partial_transform",
    )(val_idx,con_idx,e_val,e_con,pv,pc,gmap.reshape(32,128),jnp.asarray(z_tables()),jnp.asarray(x_tables()))

def body(psi_val, psi_con, e_val, e_con, val_idx, con_idx, gmap):
    part,w=partial_transform(val_idx,con_idx,e_val,e_con,psi_val,psi_con,gmap)
    recv=lax.all_to_all(part,("row","col"),split_axis=0,concat_axis=0,tiled=True)
    own=recv.astype(jnp.float32).sum(0).astype(jnp.bfloat16)
    every=lax.all_gather(own,"col",axis=0)
    weighted=(every.astype(jnp.float32)*w[None,:,:1]).astype(jnp.bfloat16)
    rowside=weighted.reshape(4,16,2,512).transpose(0,2,1,3).reshape(8,1,16,512)
    colside=own.reshape(16,2,512).transpose(1,0,2).reshape(1,2,16,512)
    payload=jnp.concatenate([jnp.broadcast_to(colside,(8,2,16,512)),jnp.broadcast_to(rowside,(8,2,16,512))],axis=3).reshape(16,16,1024)
    groups=lax.all_to_all(payload,("ph","pl"),split_axis=0,concat_axis=0,tiled=True).reshape(256,1024)
    tiles=lax.dot_general(groups[:,512:],groups[:,:512],(((0,),(0,)),((),())),preferred_element_type=jnp.float32).astype(jnp.bfloat16)
    tiles=lax.all_to_all(tiles.reshape(8,64,512),("pl","row"),split_axis=0,concat_axis=0,tiled=True)
    sums=tiles.reshape(2,4,64,512).astype(jnp.float32).sum(1)
    return jnp.concatenate([sums[0],sums[1]],axis=1)

def solution(mesh):
    fine=Mesh(mesh.devices.reshape(8,2,4,4),("ph","pl","row","col"))
    pair=("ph","pl")
    return jax.shard_map(
        body,
        mesh=fine,
        in_specs=(
            P(None, ("row", "col")),
            P(None, ("row", "col")),
            P(),
            P(),
            P(pair),
            P(pair),
            P(),
        ),
        out_specs=P(("ph","pl","row"), "col"),
        check_vma=False,
    )
```

```python
import math
import numpy as np
import jax, jax.numpy as jnp
from jax import lax
from jax.experimental import pallas as pl
from jax.experimental.pallas import tpu as pltpu
from jax.sharding import Mesh, PartitionSpec as P
import ml_dtypes
BF=ml_dtypes.bfloat16
GX=64;GY=64;GZ=192;NG=4096
KZ=104

def split_hi_lo(t):
    hi=t.astype(np.float32).astype(BF); lo=(t-hi.astype(np.float64)).astype(np.float32).astype(BF)
    return hi,lo

def z_tables():
    z=np.arange(GZ); k=np.arange(97)
    ang=2*np.pi/GZ*((k[:,None]*z[None,:])%GZ)
    t=np.zeros((2,KZ,GZ)); t[0,:97]=np.cos(ang); t[1,:97]=-np.sin(ang)
    t=t.reshape(2*KZ,GZ)
    out=np.zeros((2,4*KZ,256),BF)
    hi,lo=split_hi_lo(t)
    for par,off in ((0,0),(1,64)):
        out[par,:2*KZ,off:off+GZ]=hi; out[par,2*KZ:,off:off+GZ]=lo
    return out

def x_tables():
    factor=1.0/math.sqrt(GX*GY*GZ)
    out=np.zeros((16,16,256),BF)
    fx=np.arange(64)
    for d in range(16):
        xs=4*d+np.arange(4)
        ang=2*np.pi/GX*((fx[None,:]*xs[:,None])%GX)
        c=np.cos(ang)*factor; s=np.sin(ang)*factor
        for f,sig in ((0,1.0),(1,-1.0)):
            t=np.concatenate([c,sig*s,sig*c,-s],axis=0)
            hi,lo=split_hi_lo(t)
            out[d,:,f*64:(f+1)*64]=hi; out[d,:,128+f*64:128+(f+1)*64]=lo
    return out

def fft8(v):
    def add(a,b): return (a[0]+b[0],a[1]+b[1])
    def sub(a,b): return (a[0]-b[0],a[1]-b[1])
    def addmi(a,b): return (a[0]+b[1],a[1]-b[0])
    def submi(a,b): return (a[0]-b[1],a[1]+b[0])
    r=np.float32(math.sqrt(0.5))
    def fft4(x0,x1,x2,x3):
        a=add(x0,x2); b=sub(x0,x2); c=add(x1,x3); d=sub(x1,x3)
        return add(a,c),addmi(b,d),sub(a,c),submi(b,d)
    e=fft4(v[0],v[2],v[4],v[6]); o=fft4(v[1],v[3],v[5],v[7])
    o1=((o[1][0]+o[1][1])*r,(o[1][1]-o[1][0])*r)
    o3=((o[3][1]-o[3][0])*r,(o[3][0]+o[3][1])*(-r))
    return [add(e[0],o[0]),add(e[1],o1),addmi(e[2],o[2]),add(e[3],o3),
            sub(e[0],o[0]),sub(e[1],o1),submi(e[2],o[2]),sub(e[3],o3)]

def transform_kernel(val_s, con_s, ev_s, ec_s, pv, pc, gmaps, ztabs, xtabs, out, wout, va, vb, gmap, ztab, rho, Z, Z2, GA, GB, xtab, rows_v, kcode, row_s, asem, bsem, gsem, zsem, xsem, rsem):
    place=lax.axis_index("row")*4+lax.axis_index("col")
    planes=[(pltpu.make_async_copy(pv.at[:,pl.ds(12288*x,12288)],va.at[x],asem.at[x]),
             pltpu.make_async_copy(pc.at[:,pl.ds(12288*x,12288)],vb.at[x],bsem.at[x])) for x in range(4)]
    small=pltpu.make_async_copy(gmaps,gmap,gsem)
    small.start()
    for one in planes:
        one[0].start()
        one[1].start()
    fetch=pltpu.make_async_copy(xtabs.at[place],xtab,xsem)
    fetch.start()
    table=pltpu.make_async_copy(ztabs,ztab,zsem)
    table.start()
    small.wait()
    g=gmap[...]
    q=((g.astype(jnp.float32)+0.5)*np.float32(1.0/GZ)).astype(jnp.int32)
    fz=g-q*GZ; fy=q&63; fx=q>>6
    flip=fz>96
    fz=jnp.where(flip,GZ-fz,fz)
    fy=jnp.where(flip,(64-fy)&63,fy)
    rows_v[...]=((fy&7)*8+(fy>>3))*(2*KZ)+2*fz
    kcode[...]=jnp.where(flip,64,0)+fx
    move=pltpu.make_async_copy(rows_v,row_s,rsem)
    move.start()
    first=lax.axis_index("row")*8
    pid=lax.broadcasted_iota(jnp.int32,(16,128),0)%8
    ev=jnp.zeros((16,128),jnp.float32); ec=jnp.ones((16,128),jnp.float32)
    for p in range(8):
        ev=jnp.where(pid==p,ev_s[val_s[first+p]],ev)
        ec=jnp.where(pid==p,ec_s[con_s[first+p]],ec)
    wout[...]=-2.0/(math.sqrt(512)*(ec-ev))
    sub=lax.broadcasted_iota(jnp.int32,(8,96),0); lane=lax.broadcasted_iota(jnp.int32,(8,96),1)
    picks=[]
    for q in range(8):
        want=jnp.zeros((8,96),jnp.int32)
        for k in range(8):
            p=8*q+k
            want=jnp.where(sub==k, val_s[p] if p<32 else con_s[p-32]+32, want)
        picks.append((want==lane).astype(jnp.float32))
    sel=jnp.concatenate(picks,axis=0).astype(jnp.bfloat16)
    CH=512
    for x in range(4):
        planes[x][0].wait()
        planes[x][1].wait()
        for u in range(12288//CH):
            o=u*CH
            src=jnp.concatenate([va[x,:,o:o+CH],vb[x,:,o:o+CH]],axis=0)
            res=jnp.dot(sel,src,preferred_element_type=jnp.float32)
            rho[x,:,o:o+CH]=(res[:32]*res[32:]).astype(jnp.bfloat16)
    fetch.wait()
    table.wait()
    move.wait()
    for b in range(8):
        wt=ztab[b%2]
        for ah in range(0,8,2):
            parts=[]
            for a in range(ah,ah+2):
                o=384*(4*a+b//2)+128*(b%2)
                for x in range(4):
                    parts.append(rho[x,:,o:o+256])
            B=jnp.concatenate(parts,axis=0)
            res=lax.dot_general(wt,B,(((1,),(1,)),((),())),preferred_element_type=jnp.float32)
            res=res[:2*KZ]+res[2*KZ:]
            for a in range(2):
                Z[pl.ds((8*(ah+a)+b)*2*KZ,2*KZ),:]=res[:,128*a:128*a+128]
    tw=[[np.exp(-2j*np.pi*b*k/64) for k in range(8)] for b in range(8)]
    def pass1(j,_):
        r0=pl.multiple_of(j*8,8)
        for b in range(8):
            v=[(Z[pl.ds((8*a+b)*2*KZ+r0,8),:],Z[pl.ds((8*a+b)*2*KZ+KZ+r0,8),:]) for a in range(8)]
            w=fft8(v)
            for k in range(8):
                re,im=w[k]
                if b and k:
                    c=np.float32(tw[b][k].real); s=np.float32(tw[b][k].imag)
                    re,im=re*c-im*s, re*s+im*c
                Z[pl.ds((8*k+b)*2*KZ+r0,8),:]=re; Z[pl.ds((8*k+b)*2*KZ+KZ+r0,8),:]=im
        return 0
    lax.fori_loop(0,KZ//8,pass1,0,unroll=True)
    def pass2(j,_):
        r0=pl.multiple_of(j*8,8)
        for k1 in range(8):
            v=[(Z[pl.ds((8*k1+b)*2*KZ+r0,8),:],Z[pl.ds((8*k1+b)*2*KZ+KZ+r0,8),:]) for b in range(8)]
            w=fft8(v)
            for k in range(8):
                re,im=w[k]
                base=(8*k1+k)*2*KZ+2*r0
                Z2[pl.ds(base,8,stride=2),:]=re; Z2[pl.ds(base+1,8,stride=2),:]=im
        return 0
    lax.fori_loop(0,KZ//8,pass2,0)
    ksub=lax.broadcasted_iota(jnp.int32,(128,128),0)
    def gather(t,G):
        for j in range(256):
            rr=pl.multiple_of(row_s[2*t+j//128,j%128],2)
            G[pl.ds(2*j,2),:]=Z2[pl.ds(rr,2),:]
    def phase(t,G):
        c=t//4
        for h in range(2):
            oh=(ksub==kcode[pl.ds(2*t+h,1),:]).astype(jnp.bfloat16)
            oh=jnp.concatenate([oh,oh],axis=0)
            co=jnp.dot(xtab[...],oh,preferred_element_type=jnp.float32)
            R=G[pl.ds(256*h,128,stride=2),:].T; I=G[pl.ds(256*h+1,128,stride=2),:].T
            re=0.0; im=0.0
            for x in range(4):
                rx=R[32*x:32*x+32]; ix=I[32*x:32*x+32]
                re=re+co[x:x+1]*rx+co[4+x:5+x]*ix
                im=im+co[8+x:9+x]*ix+co[12+x:13+x]*rx
            at=pl.multiple_of((t%4)*256+h*128,128)
            for r in range(4):
                both=jnp.concatenate([re[8*r:8*r+8],im[8*r:8*r+8]],axis=0)
                out[r*4+c,:,pl.ds(at,128)]=both.astype(jnp.bfloat16)
    gather(0,GA)
    for t in range(16):
        if t<15:
            gather(t+1,(GA,GB)[(t+1)%2])
        phase(t,(GA,GB)[t%2])

def partial_transform(val_idx,con_idx,e_val,e_con,pv,pc,gmap):
    smem=pl.BlockSpec(memory_space=pltpu.SMEM)
    return pl.pallas_call(
        transform_kernel,
        grid=(1,),
        in_specs=[smem,smem,smem,smem,
                  pl.BlockSpec(memory_space=pl.ANY),
                  pl.BlockSpec(memory_space=pl.ANY),
                  pl.BlockSpec(memory_space=pl.ANY),
                  pl.BlockSpec(memory_space=pl.ANY),
                  pl.BlockSpec(memory_space=pl.ANY)],
        out_specs=[pl.BlockSpec((16,16,1024),lambda i:(0,0,0)),pl.BlockSpec((16,128),lambda i:(0,0))],
        scratch_shapes=[pltpu.VMEM((4,32,12288),jnp.bfloat16),
                        pltpu.VMEM((4,64,12288),jnp.bfloat16),
                        pltpu.VMEM((32,128),jnp.int32),
                        pltpu.VMEM((2,4*KZ,256),jnp.bfloat16),
                        pltpu.VMEM((4,32,12288),jnp.bfloat16),
                        pltpu.VMEM((64*2*KZ,128),jnp.float32),
                        pltpu.VMEM((64*2*KZ,128),jnp.float32),
                        pltpu.VMEM((512,128),jnp.float32),
                        pltpu.VMEM((512,128),jnp.float32),
                        pltpu.VMEM((16,256),jnp.bfloat16),
                        pltpu.VMEM((32,128),jnp.int32),
                        pltpu.VMEM((32,128),jnp.int32),
                        pltpu.SMEM((32,128),jnp.int32),
                        pltpu.SemaphoreType.DMA((4,)),
                        pltpu.SemaphoreType.DMA((4,)),
                        pltpu.SemaphoreType.DMA,
                        pltpu.SemaphoreType.DMA,
                        pltpu.SemaphoreType.DMA,
                        pltpu.SemaphoreType.DMA],
        out_shape=[jax.ShapeDtypeStruct((16,16,1024),jnp.bfloat16),jax.ShapeDtypeStruct((16,128),jnp.float32)],
        compiler_params=pltpu.CompilerParams(vmem_limit_bytes=60*2**20, dimension_semantics=("arbitrary",)),
        name="partial_transform",
    )(val_idx,con_idx,e_val,e_con,pv,pc,gmap.reshape(32,128),jnp.asarray(z_tables()),jnp.asarray(x_tables()))

def body(psi_val, psi_con, e_val, e_con, val_idx, con_idx, gmap):
    part,w=partial_transform(val_idx,con_idx,e_val,e_con,psi_val,psi_con,gmap)
    recv=lax.all_to_all(part,("row","col"),split_axis=0,concat_axis=0,tiled=True)
    own=recv.astype(jnp.float32).sum(0).astype(jnp.bfloat16)
    every=lax.all_gather(own,"col",axis=0)
    weighted=(every.astype(jnp.float32)*w[None,:,:1]).astype(jnp.bfloat16)
    rowside=weighted.reshape(4,16,2,512).transpose(0,2,1,3).reshape(8,1,16,512)
    colside=own.reshape(16,2,512).transpose(1,0,2).reshape(1,2,16,512)
    payload=jnp.concatenate([jnp.broadcast_to(colside,(8,2,16,512)),jnp.broadcast_to(rowside,(8,2,16,512))],axis=3).reshape(16,16,1024)
    groups=lax.all_to_all(payload,("ph","pl"),split_axis=0,concat_axis=0,tiled=True).reshape(256,1024)
    tiles=lax.dot_general(groups[:,512:],groups[:,:512],(((0,),(0,)),((),())),preferred_element_type=jnp.float32).astype(jnp.bfloat16)
    tiles=lax.all_to_all(tiles.reshape(8,64,512),("pl","row"),split_axis=0,concat_axis=0,tiled=True)
    sums=tiles.reshape(2,4,64,512).astype(jnp.float32).sum(1)
    return jnp.concatenate([sums[0],sums[1]],axis=1)

def solution(mesh):
    fine=Mesh(mesh.devices.reshape(8,2,4,4),("ph","pl","row","col"))
    pair=("ph","pl")
    return jax.shard_map(
        body,
        mesh=fine,
        in_specs=(
            P(None, ("row", "col")),
            P(None, ("row", "col")),
            P(),
            P(),
            P(pair),
            P(pair),
            P(),
        ),
        out_specs=P(("ph","pl","row"), "col"),
        check_vma=False,
    )
```
